256 devices in a mesh: pipe: 16 (over z_lo, x, core), expert: 16 (over z_hi, y).
Axes of the slice: x: 4, y: 4, z: 8 (z_hi: 4, z_lo: 2; z = z_hi * 2 + z_lo), core: 2. Of those that a mesh axis runs over, the one named last changes fastest.
Arguments:
- front_rows: bfloat16 [16, 1024, 3584], P('pipe', 'expert'), may hold values from -6 to 6
- front_grad: bfloat16 [16, 1024, 3584], P('pipe', 'expert'), may hold values from -6 to 6
- front_routes: int32 [16, 1024, 4], P('pipe', 'expert'), may hold values from 0 to 7, all different within a row; in each aligned block of 64 rows (0 to 63, 64 to 127, ..., all dimensions but the last counted through in order) at most 36 rows name the same one
- front_logits: bfloat16 [16, 1024, 4], P('pipe', 'expert'), may hold values from -6 to 6
- rear_rows: bfloat16 [16, 1024, 3584], P('pipe', 'expert'), may hold values from -6 to 6
- rear_grad: bfloat16 [16, 1024, 3584], P('pipe', 'expert'), may hold values from -6 to 6
- rear_routes: int32 [16, 1024, 4], P('pipe', 'expert'), may hold values from 0 to 7, all different within a row; in each aligned block of 64 rows (0 to 63, 64 to 127, ..., all dimensions but the last counted through in order) at most 36 rows name the same one
- rear_logits: bfloat16 [16, 1024, 4], P('pipe', 'expert'), may hold values from -6 to 6
- up_weight: bfloat16 [16, 3584, 8192], P('pipe', None, 'expert'), may hold values from -0.09375 to 0.09375
- down_weight: bfloat16 [16, 8192, 3584], P('pipe', 'expert'), may hold values from -0.1875 to 0.1875
Outputs:
- front_input_grad: bfloat16 [16, 1024, 3584], P('pipe', 'expert')
- rear_input_grad: bfloat16 [16, 1024, 3584], P('pipe', 'expert')
- down_grad: bfloat16 [16, 8192, 3584], P('pipe', 'expert')
The draws below stay inside these ranges and needn't reach their ends.
Inputs may be any that keep to these rules, and one draw needn't show every extreme that they name: `front_routes`: each row names 4 different experts. In the rows of one device (aligned blocks of 64 rows within one pipe index), no expert is named by more than 36 rows, a bound that some block reaches. `rear_routes`: as for front_routes.
All inputs are finite; a program needn't handle non-finite values.
Results may differ from the reference program's by a relative error of at most 0.01.
Values may be sent and summed in bfloat16 or wider, within the bound.
A program may use at most 128 MiB of HBM per device.

```python
import math
import jax
import jax.numpy as jnp
import numpy as np
from jax import lax

D = 3584
FF = 1024
EXPERTS = 8
TOP = 4
HIDDEN_GROUPS = 2
TOK_DEV = 64
CAP = 36
TOKENS = 1024
SECTIONS = 16
N_EXPERT = 16


def block_levels(key, dims, split, smallest, high):
    loudness, own = 1.0, jax.random.fold_in(key, 6)
    for dim, blocks in split:
        steps = jnp.exp(jax.random.uniform(jax.random.fold_in(own, dim), (blocks,), jnp.float32, smallest / len(split), high / len(split)))
        loudness = loudness * jnp.repeat(steps, dims[dim] // blocks).reshape([-1 if axis == dim else 1 for axis in range(len(dims))])
    return loudness


def routed_block(own_key, own, number, rows, number_of, top, reach, skew):
    sequence = jax.random.permutation(own_key, number_of)
    crowded, ordinary = portions_of(number_of, rows * top, reach, skew, True), portions_of(number_of, rows * top, reach, skew, False)
    places = jnp.arange(number_of)

    def named(tallies, turn):
        used = int((tallies > 0).sum())
        fixed = max(1, used // 4)
        passed = fixed + (places - fixed + turn * (used - fixed)) % max(1, number_of - fixed)
        return jnp.zeros((number_of,), jnp.int32).at[sequence[jnp.where(places < fixed, places, passed)]].set(jnp.asarray(tallies, jnp.int32))

    tallies = jnp.where(number % 4 == 0, named(crowded, number // 4), named(ordinary, number - number // 4 - 1))
    mixed = jax.random.permutation(jax.random.fold_in(own, 3), number_of)
    donor, taker = mixed[0:number_of // 2 * 2:2], mixed[1:number_of // 2 * 2:2]
    margin = jnp.minimum(tallies[donor] - 1, reach - tallies[taker]) // 2
    margin = jnp.where((donor == sequence[0]) | (taker == sequence[0]) | (tallies[taker] == 0), 0, jnp.maximum(margin, 0))
    passed = jax.random.randint(jax.random.fold_in(own, 4), (number_of // 2,), 0, 1 << 20) % (margin + 1)
    tallies = tallies.at[donor].add(-passed).at[taker].add(passed)
    items = jnp.searchsorted(jnp.cumsum(tallies), jnp.arange(rows * top), side="right").astype(jnp.int32)
    table = items.reshape(top, rows).T
    table = table[jax.random.permutation(jax.random.fold_in(own, 1), rows)]
    turn = jax.random.randint(jax.random.fold_in(own, 2), (rows, 1), 0, top)
    return jnp.take_along_axis(table, (jnp.arange(top)[None, :] + turn) % top, axis=1)


def portions_of(count, total, most, lean, full):
    loads = [(1 << 20) // math.isqrt(grade ** lean) + 1 for grade in range(1, count + 1)]
    largest = most if full else min(most, max(-(-total // count), total * loads[0] // sum(loads)))
    least = 1 if total - largest >= count - 1 else 0
    holding, spare = [largest] + [least] * (count - 1), total - largest - least * (count - 1)
    while spare > 0:
        free = [i for i in range(1, count) if holding[i] < largest] or [i for i in range(1, count) if holding[i] < most]
        mass, left = sum([loads[i] for i in free]), spare
        for i in free:
            addition = min(most - holding[i], max(1, left * loads[i] // mass), spare)
            holding[i] = holding[i] + addition
            spare = spare - addition
    return np.array(holding)


def noise(rng, dims, width, bound, cuts=(), kind=jnp.bfloat16):
    entries = width * jax.random.normal(rng, dims, jnp.float32)
    if cuts:
        entries = entries * block_levels(rng, dims, cuts, -0.22, 0.18)
    return jnp.clip(entries, -bound, bound).astype(kind)


def setup_inputs(seed: int = 0) -> dict:
    seeds = jax.random.split(jax.random.key(seed), 11)
    front_rows = noise(seeds[0], (SECTIONS, TOKENS, D), 1.0, 6.0, ((0, 16), (1, 16)))
    front_grad = noise(seeds[1], (SECTIONS, TOKENS, D), 1.0, 6.0, ((0, 16), (1, 16)))
    front_routes_keys = jax.random.split(jax.random.fold_in(seeds[2], 1), SECTIONS * TOKENS // TOK_DEV)
    front_routes_turns = jax.random.permutation(jax.random.fold_in(seeds[2], 3), SECTIONS * TOKENS // TOK_DEV)
    front_routes = jax.vmap(lambda own, number: routed_block(jax.random.fold_in(seeds[2], 2), own, number, TOK_DEV, EXPERTS, TOP, CAP, 2))(front_routes_keys, front_routes_turns).reshape((SECTIONS, TOKENS, TOP))
    front_logits = noise(seeds[3], (SECTIONS, TOKENS, TOP), 1.5, 6.0, ((0, 16), (1, 16)))
    rear_rows = noise(seeds[4], (SECTIONS, TOKENS, D), 1.0, 6.0, ((0, 16), (1, 16)))
    rear_grad = noise(seeds[5], (SECTIONS, TOKENS, D), 1.0, 6.0, ((0, 16), (1, 16)))
    rear_routes_keys = jax.random.split(jax.random.fold_in(seeds[6], 1), SECTIONS * TOKENS // TOK_DEV)
    rear_routes_turns = jax.random.permutation(jax.random.fold_in(seeds[6], 3), SECTIONS * TOKENS // TOK_DEV)
    rear_routes = jax.vmap(lambda own, number: routed_block(jax.random.fold_in(seeds[6], 2), own, number, TOK_DEV, EXPERTS, TOP, CAP, 2))(rear_routes_keys, rear_routes_turns).reshape((SECTIONS, TOKENS, TOP))
    rear_logits = noise(seeds[7], (SECTIONS, TOKENS, TOP), 1.5, 6.0, ((0, 16), (1, 16)))
    up_weight = noise(seeds[8], (SECTIONS, D, EXPERTS * FF), D ** -0.5, 0.09375, ((0, 16), (2, 16)))
    down_weight = noise(seeds[9], (SECTIONS, EXPERTS * FF, D), FF ** -0.5, 0.1875, ((0, 16), (1, 16)))
    return dict(front_rows=front_rows, front_grad=front_grad, front_routes=front_routes, front_logits=front_logits, rear_rows=rear_rows, rear_grad=rear_grad, rear_routes=rear_routes, rear_logits=rear_logits, up_weight=up_weight, down_weight=down_weight)


epsilon = 1e-06
HIGHEST_PRECISION = lax.Precision.HIGHEST

def gate_table(routes, logits):
    weights = jax.nn.sigmoid(logits.astype(jnp.float32))
    weights = (weights / lax.optimization_barrier(jnp.sum(weights, axis=-1, keepdims=True))).astype(jnp.bfloat16)
    onehot = routes[..., None] == jnp.arange(EXPERTS, dtype=jnp.int32)
    picked = jnp.where(onehot, weights[..., None].astype(jnp.float32), jnp.float32(0.0))
    return lax.optimization_barrier(jnp.sum(picked, axis=-2)).astype(jnp.bfloat16)

def slot_positions(gate_grid, routes):
    chosen = (gate_grid != 0).astype(jnp.int32)
    blocks = chosen.reshape(N_EXPERT, TOK_DEV, EXPERTS)
    slot_rank = jnp.cumsum(blocks, axis=1) - blocks
    offset = jnp.arange(N_EXPERT, dtype=jnp.int32)[:, None, None] * CAP
    grid = (slot_rank + offset).reshape(TOKENS, EXPERTS).astype(jnp.int32)
    return jnp.take_along_axis(grid, routes, axis=1).astype(jnp.int32)

def normalize(row_block):
    rows_float = row_block.astype(jnp.float32)
    inv_rms = lax.rsqrt(lax.optimization_barrier(jnp.mean(rows_float * rows_float, axis=-1, keepdims=True)) + epsilon)
    return (rows_float, inv_rms, (rows_float * inv_rms).astype(jnp.bfloat16))

def spread(values, routes, slots):
    buffer = jnp.zeros((EXPERTS, N_EXPERT * CAP, values.shape[-1]), values.dtype)
    return buffer.at[routes, slots].set(values)

def rounded(values):
    return lax.optimization_barrier(values.astype(jnp.bfloat16)).astype(jnp.float32)

def section_backward(row_block, incoming, routes, logits, up_section, down_section):
    grid = gate_table(routes, logits)
    slots = slot_positions(grid, routes)
    gates = jnp.take_along_axis(grid, routes, axis=1).astype(jnp.float32)
    rows_float, inv_rms, normed = normalize(row_block)
    gated = (gates[..., None] * incoming.astype(jnp.float32)[:, None, :]).astype(jnp.bfloat16)
    spread_rows = spread(jnp.broadcast_to(normed[:, None, :], (TOKENS, TOP, D)), routes, slots).astype(jnp.float32)
    spread_grads = spread(gated, routes, slots).astype(jnp.float32)
    up_float = up_section.astype(jnp.float32).reshape(D, EXPERTS, FF)
    pre_act = jnp.einsum('esd,def->esf', spread_rows, up_float, precision=HIGHEST_PRECISION)
    sigmoid_pre = jax.nn.sigmoid(pre_act)
    hidden = rounded(pre_act * sigmoid_pre)
    grad_down = jnp.einsum('esf,esd->efd', hidden, spread_grads, precision=HIGHEST_PRECISION)
    grad_down = grad_down.reshape(EXPERTS * FF, D).astype(jnp.bfloat16)
    down_float = down_section.astype(jnp.float32).reshape(EXPERTS, FF, D)
    grad_hidden = jnp.einsum('esd,efd->esf', spread_grads, down_float, precision=HIGHEST_PRECISION)
    grad_pre = rounded(grad_hidden * sigmoid_pre * (1.0 + pre_act * (1.0 - sigmoid_pre)))
    group_width = FF // HIDDEN_GROUPS
    grad_groups = grad_pre.reshape(EXPERTS, N_EXPERT * CAP, HIDDEN_GROUPS, group_width)
    up_groups = up_float.reshape(D, EXPERTS, HIDDEN_GROUPS, group_width)
    pieces = rounded(jnp.einsum('esgf,degf->egsd', grad_groups, up_groups, precision=HIGHEST_PRECISION))
    grad_spread = lax.optimization_barrier(jnp.sum(pieces, axis=1))
    grad_normed = lax.optimization_barrier(jnp.sum(grad_spread[routes, slots], axis=1))
    inner = lax.optimization_barrier(jnp.sum(grad_normed * rows_float, axis=-1, keepdims=True)) / rows_float.shape[-1]
    grad_rows = inv_rms * grad_normed - inv_rms * inv_rms * inv_rms * rows_float * inner
    return ((incoming.astype(jnp.float32) + grad_rows).astype(jnp.bfloat16), grad_down)

def reference(front_rows, front_grad, front_routes, front_logits, rear_rows, rear_grad, rear_routes, rear_logits, up_weight, down_weight):
    indices = jnp.arange(SECTIONS, dtype=jnp.int32)
    partner = (indices + 1 - 2 * (indices % 2)).astype(jnp.int32)

    def run_section(operands):
        rows, grads, routes, logits, which = operands
        return section_backward(rows, grads, routes, logits, up_weight[which], down_weight[which])
    front_input_grad, front_down = lax.map(run_section, (front_rows, front_grad, front_routes, front_logits, indices))
    rear_input_grad, rear_down = lax.map(run_section, (rear_rows, rear_grad, rear_routes, rear_logits, partner))

    def add_mirror(operands):
        own, which = operands
        return (own.astype(jnp.float32) + rear_down[which].astype(jnp.float32)).astype(jnp.bfloat16)
    down_grad = lax.map(add_mirror, (front_down, partner))
    return (front_input_grad, rear_input_grad, down_grad)
```

```python
import jax
import jax.numpy as jnp
from jax import lax
from jax.sharding import PartitionSpec as P

FF = 1024
EXPERTS = 8
CAP = 36
NY = 4
NZ = 4
TOK = 64
PAD = 128

epsilon = 1e-06


def gate_table(routes, logits):
    weights = jax.nn.sigmoid(logits.astype(jnp.float32))
    weights = (weights / jnp.sum(weights, axis=-1, keepdims=True)).astype(jnp.bfloat16)
    onehot = routes[..., None] == jnp.arange(EXPERTS, dtype=jnp.int32)
    picked = jnp.where(onehot, weights[..., None].astype(jnp.float32), jnp.float32(0.0))
    return jnp.sum(picked, axis=-2).astype(jnp.bfloat16)


def normalize(row_block):
    rows_float = row_block.astype(jnp.float32)
    inv_rms = lax.rsqrt(jnp.mean(rows_float * rows_float, axis=-1, keepdims=True) + epsilon)
    return (rows_float, inv_rms, (rows_float * inv_rms).astype(jnp.bfloat16))


def move_y(x, to):
    return lax.ppermute(x, "expert", [(z * NY + y, z * NY + to(y)) for z in range(NZ) for y in range(NY)])


def move_z(x, by):
    return lax.ppermute(x, "expert", [(z * NY + y, (z + by) % NZ * NY + y) for z in range(NZ) for y in range(NY)])


def swap_core(x):
    return lax.ppermute(x, "pipe", [(i, i ^ 1) for i in range(lax.axis_size("pipe"))])


def serves(y):
    return 1 if y in (1, 2) else 0


def swap_weights(x):
    pairs = []
    for p in range(lax.axis_size("pipe")):
        for i in range(16):
            y, core = i % NY, p % 2
            if core == serves(y):
                pairs.append((p * 16 + i, p * 16 + i))
            else:
                pairs.append((p * 16 + i, (p ^ 1) * 16 + (i ^ 1)))
    return lax.ppermute(x, ("pipe", "expert"), pairs)


def pick(table, expert):
    gate = lax.dynamic_index_in_dim(table, expert, axis=2, keepdims=False)
    chosen = (gate != 0).astype(jnp.int32)
    rank = jnp.cumsum(chosen, axis=1) - chosen
    slots = jnp.arange(CAP, dtype=jnp.int32)[None, :, None]
    picks = ((chosen[:, None, :] == 1) & (rank[:, None, :] == slots)).astype(jnp.bfloat16)
    return picks, picks * gate[:, None, :]


def packed(payload, expert, width):
    blocks = payload.reshape(-1, TOK, payload.shape[-1])
    picks, weighted = pick(blocks[:, :, 2 * width : 2 * width + EXPERTS], expert)
    rows = jnp.einsum("bct,btd->bcd", picks, blocks[:, :, :width], preferred_element_type=jnp.float32)
    grads = jnp.einsum(
        "bct,btd->bcd", weighted, blocks[:, :, width : 2 * width], preferred_element_type=jnp.float32
    )
    return picks, jnp.stack([rows, grads]).astype(jnp.bfloat16).reshape(2, -1, width)


def expert_rows(rows, grads, up, down):
    hidden, grad_pre = [], []
    for u, d in zip(up, down):
        pre = jnp.dot(rows, u, preferred_element_type=jnp.float32)
        s = jax.nn.sigmoid(pre)
        hidden.append((pre * s).astype(jnp.bfloat16))
        grad_hidden = lax.dot_general(grads, d, (((1,), (1,)), ((), ())), preferred_element_type=jnp.float32)
        grad_pre.append((grad_hidden * s * (1.0 + pre * (1.0 - s))).astype(jnp.bfloat16))
    total = sum(
        lax.dot_general(g, u, (((1,), (1,)), ((), ())), preferred_element_type=jnp.float32)
        for g, u in zip(grad_pre, up)
    )
    return hidden, total.astype(jnp.bfloat16)


def finish(rows_float, inv_rms, incoming, grad_normed):
    grad_normed = grad_normed.astype(jnp.float32)
    inner = jnp.sum(grad_normed * rows_float, axis=-1, keepdims=True) / rows_float.shape[-1]
    grad_rows = inv_rms * grad_normed - inv_rms * inv_rms * inv_rms * rows_float * inner
    return (incoming.astype(jnp.float32) + grad_rows).astype(jnp.bfloat16)


def on_device(fx, fg, froutes, flogits, rx, rg, rroutes, rlogits, up_weight, down_weight):
    width = fx.shape[-1]
    core = lax.axis_index("pipe") % 2
    place = lax.axis_index("expert")
    y, z = place % NY, place // NY
    served = ((y == 1) | (y == 2)).astype(jnp.int32)
    front_stays = core == served
    mine, other = 2 * z + y // 2, 2 * z + 1 - y // 2

    up_a = swap_weights(up_weight[0])
    down_a = swap_weights(down_weight[0])
    up_b, down_b = swap_core(up_a), swap_core(down_a)

    both = []
    for x, g, routes, logits in ((fx, fg, froutes, flogits), (rx, rg, rroutes, rlogits)):
        rows_float, inv_rms, normed = normalize(x[0])
        table = jnp.pad(gate_table(routes[0], logits[0]), ((0, 0), (0, PAD - EXPERTS)))
        both.append((rows_float, inv_rms, g[0], jnp.concatenate([normed, g[0], table], axis=1)))
    kept = jnp.where(front_stays, both[0][3], both[1][3])
    sent = jnp.where(front_stays, both[1][3], both[0][3])

    shard = jnp.concatenate([kept, move_y(sent, lambda v: v ^ 1)], axis=0)
    from_below, from_above = move_z(shard, 1), move_z(shard, -1)
    across = jnp.concatenate([move_z(from_below[:TOK], 1), move_z(from_above[TOK:], -1)], axis=0)

    chunks = []
    for payload in (shard, jnp.concatenate([from_below, from_above], axis=0), across):
        picks_other, packed_other = packed(payload, other, width)
        arrived = move_y(packed_other, lambda v: 3 - v)
        picks_mine, packed_mine = packed(payload, mine, width)
        chunks.append((picks_mine, picks_other, jnp.concatenate([packed_mine, arrived], axis=1)))

    hiddens, partials = [], []
    for picks_mine, picks_other, rows in chunks:
        hidden, pieces = expert_rows(rows[0], rows[1], (up_a, up_b), (down_a, down_b))
        hiddens.append(hidden)
        half = pieces.shape[0] // 2
        back = move_y(pieces[half:], lambda v: 3 - v)
        total = jnp.einsum(
            "bct,bcd->btd", picks_mine, pieces[:half].reshape(-1, CAP, width), preferred_element_type=jnp.float32
        ) + jnp.einsum(
            "bct,bcd->btd", picks_other, back.reshape(-1, CAP, width), preferred_element_type=jnp.float32
        )
        partials.append(total.reshape(-1, width))
    own, near, far = partials
    far = far.astype(jnp.bfloat16)
    half_down, half_up = move_z(far[:TOK], -1), move_z(far[TOK:], 1)
    below, above = near[: 2 * TOK], near[2 * TOK :]
    below = jnp.concatenate([below[:TOK] + half_down.astype(jnp.float32), below[TOK:]], axis=0)
    above = jnp.concatenate([above[:TOK], above[TOK:] + half_up.astype(jnp.float32)], axis=0)
    back_a = move_z(below.astype(jnp.bfloat16), -1)
    back_b = move_z(above.astype(jnp.bfloat16), 1)
    total = own + back_a.astype(jnp.float32) + back_b.astype(jnp.float32)
    returned = move_y(total[TOK:].astype(jnp.bfloat16), lambda v: v ^ 1).astype(jnp.float32)
    results = []
    for stays, (rows_float, inv_rms, g, _) in zip((front_stays, ~front_stays), both):
        results.append(finish(rows_float, inv_rms, g, jnp.where(stays, total[:TOK], returned)))

    grads = jnp.concatenate([c[2][1] for c in chunks], axis=0)
    down_parts = [
        lax.dot_general(
            jnp.concatenate([h[i] for h in hiddens], axis=0),
            grads,
            (((0,), (0,)), ((), ())),
            preferred_element_type=jnp.float32,
        ).astype(jnp.bfloat16)
        for i in range(2)
    ]
    mirror = swap_core(down_parts[1])
    down = (down_parts[0].astype(jnp.float32) + mirror.astype(jnp.float32)).astype(jnp.bfloat16)
    return (results[0][None], results[1][None], swap_weights(down)[None])


def solution(mesh):
    rows = P("pipe", "expert", None)
    return jax.shard_map(
        on_device,
        mesh=mesh,
        in_specs=(rows,) * 8 + (P("pipe", None, "expert"), rows),
        out_specs=(rows, rows, rows),
        check_vma=False,
    )
```

```python
import functools

import jax
import jax.numpy as jnp
from jax import lax
from jax.experimental import pallas as pl
from jax.experimental.pallas import tpu as pltpu
from jax.sharding import PartitionSpec as P

EXPERTS = 8
CAP = 36
NY = 4
NZ = 4
TOK = 64
PAIR = 2 * TOK
SLOTS = 80
PAD = 128

epsilon = 1e-06
MESH = pl.DeviceIdType.MESH
F32, BF16 = jnp.float32, jnp.bfloat16

KEPT_UP, KEPT_DN, SWAP, SWAPPED_UP, SWAPPED_DN, FAR_KEPT, FAR_SWAPPED = range(7)
PACKED = 7
BACK = 11
SUM_FAR_KEPT, SUM_FAR_SWAPPED, SUM_ABOVE_KEPT, SUM_BELOW_SWAPPED, SUM_BELOW_KEPT, SUM_ABOVE_SWAPPED = range(15, 21)
RESULT = 21
UP_A, DOWN_A, UP_B, DOWN_B = range(22, 26)
MIRROR = 26


def gate_table(routes, logits):
    weights = jax.nn.sigmoid(logits.astype(F32))
    weights = (weights / jnp.sum(weights, axis=-1, keepdims=True)).astype(BF16)
    onehot = routes[..., None] == jnp.arange(EXPERTS, dtype=jnp.int32)
    picked = jnp.where(onehot, weights[..., None].astype(F32), F32(0.0))
    return jnp.sum(picked, axis=-2).astype(BF16)


def normalize(row_block):
    rows_float = row_block.astype(F32)
    inv_rms = lax.rsqrt(jnp.mean(rows_float * rows_float, axis=-1, keepdims=True) + epsilon)
    return (rows_float, inv_rms, (rows_float * inv_rms).astype(BF16))


def finish(rows_float, inv_rms, incoming, grad_normed):
    grad_normed = grad_normed.astype(F32)
    inner = jnp.sum(grad_normed * rows_float, axis=-1, keepdims=True) / rows_float.shape[-1]
    grad_rows = inv_rms * grad_normed - inv_rms * inv_rms * inv_rms * rows_float * inner
    return (incoming.astype(F32) + grad_rows).astype(BF16)


def tn(a, b):
    return lax.dot_general(a, b, (((0,), (0,)), ((), ())), preferred_element_type=F32)


def nt(a, b):
    return lax.dot_general(a, b, (((1,), (1,)), ((), ())), preferred_element_type=F32)


def nn(a, b):
    return lax.dot_general(a, b, (((1,), (0,)), ((), ())), preferred_element_type=F32)


def kernel(
    width, group, tile,
    kept, sent, up, down,
    out_kept, out_sent, out_down,
    tok, outbox, rows, hidden, grad_pre, picks, pieces, back, ret, retin, upw, dnw, part, mirror,
    send_sem, recv_sem, local_sem,
):
    tiles = width // tile
    pipe, place = lax.axis_index("pipe"), lax.axis_index("expert")
    core, y, z = pipe % 2, place % NY, place // NY
    served = ((y + 1) // 2) % 2
    stay = core == served
    leave = core != served
    mine, other = 2 * z + y // 2, 2 * z + 1 - y // 2
    twin = (pipe + 1 - 2 * core, place)
    beside = (pipe, z * NY + y + 1 - 2 * (y % 2))
    opposite = (pipe, z * NY + 3 - y)
    above = (pipe, ((z + 1) % NZ) * NY + y)
    below = (pipe, ((z + NZ - 1) % NZ) * NY + y)
    crossed = (twin[0], beside[1])

    barrier = pltpu.get_barrier_semaphore()
    for device in (twin, beside, opposite, above, below):
        pl.semaphore_signal(barrier, inc=1, device_id=device, device_id_type=MESH)

    @pl.when(leave)
    def _():
        pl.semaphore_signal(barrier, inc=1, device_id=crossed, device_id_type=MESH)
        pl.semaphore_wait(barrier, 6)

    @pl.when(stay)
    def _():
        pl.semaphore_wait(barrier, 5)

    def remote(index, src, dst, device):
        return pltpu.make_async_remote_copy(
            src_ref=src, dst_ref=dst, send_sem=send_sem.at[index], recv_sem=recv_sem.at[index],
            device_id=device, device_id_type=MESH,
        )

    first, second = pl.ds(0, TOK), pl.ds(TOK, TOK)
    copies = {
        KEPT_UP: remote(KEPT_UP, kept, tok.at[1, first], above),
        KEPT_DN: remote(KEPT_DN, kept, tok.at[1, second], below),
        SWAP: remote(SWAP, sent, tok.at[0, second], beside),
        SWAPPED_UP: remote(SWAPPED_UP, tok.at[0, second], tok.at[2, first], above),
        SWAPPED_DN: remote(SWAPPED_DN, tok.at[0, second], tok.at[2, second], below),
        FAR_KEPT: remote(FAR_KEPT, tok.at[1, first], tok.at[3, first], above),
        FAR_SWAPPED: remote(FAR_SWAPPED, tok.at[2, second], tok.at[3, second], below),
        SUM_FAR_KEPT: remote(SUM_FAR_KEPT, ret.at[0], retin.at[0], below),
        SUM_FAR_SWAPPED: remote(SUM_FAR_SWAPPED, ret.at[1], retin.at[1], above),
        SUM_ABOVE_KEPT: remote(SUM_ABOVE_KEPT, ret.at[2], retin.at[2], above),
        SUM_BELOW_SWAPPED: remote(SUM_BELOW_SWAPPED, ret.at[3], retin.at[3], below),
        SUM_BELOW_KEPT: remote(SUM_BELOW_KEPT, ret.at[4], retin.at[4], below),
        SUM_ABOVE_SWAPPED: remote(SUM_ABOVE_SWAPPED, ret.at[5], retin.at[5], above),
        RESULT: remote(RESULT, ret.at[6], out_sent, beside),
        UP_A: remote(UP_A, up, upw.at[0], crossed),
        DOWN_A: remote(DOWN_A, down, dnw.at[0], crossed),
        UP_B: remote(UP_B, upw.at[0], upw.at[1], twin),
        DOWN_B: remote(DOWN_B, dnw.at[0], dnw.at[1], twin),
    }
    for c in range(4):
        copies[PACKED + c] = remote(
            PACKED + c, outbox.at[pl.ds(c * SLOTS, SLOTS)], rows.at[pl.ds((2 * c + 1) * SLOTS, SLOTS)], opposite
        )
        copies[BACK + c] = remote(
            BACK + c, pieces.at[pl.ds((2 * c + 1) * SLOTS, SLOTS)], back.at[pl.ds(c * SLOTS, SLOTS)], opposite
        )
    sent_copies = []

    def start(index):
        copies[index].start()
        sent_copies.append(index)

    def arrived(index):
        copies[index].wait_recv()

    def columns(j):
        return pl.ds(pl.multiple_of(j * tile, tile), tile)

    def pack(c):
        table = tok[c, :, pl.ds(2 * width, PAD)].astype(F32)
        lane = lax.broadcasted_iota(jnp.int32, (PAIR, PAD), 1)
        later = jnp.where(lax.broadcasted_iota(jnp.int32, (PAIR, 1), 0) >= TOK, F32(CAP), F32(0.0))
        plain, weighted = [], []
        for expert in (mine, other):
            gate = jnp.sum(jnp.where(lane == expert, table, 0.0), axis=1, keepdims=True)
            rank = jnp.sum(jnp.where(lane == expert + EXPERTS, table, 0.0), axis=1, keepdims=True) + later
            hit = (gate != 0.0) & (rank == lane.astype(F32))
            plain.append(jnp.where(hit, 1.0, 0.0).astype(BF16))
            weighted.append(jnp.where(hit, gate, 0.0).astype(BF16))
        plain, weighted = jnp.concatenate(plain, axis=1), jnp.concatenate(weighted, axis=1)
        picks[c] = plain
        for part_of, matrix in ((0, plain), (width, weighted)):

            def body(j, _, part_of=part_of, matrix=matrix):
                where = pl.ds(pl.multiple_of(part_of + j * tile, 128), tile)
                got = tn(matrix, tok[c, :, where]).astype(BF16)
                rows[pl.ds(2 * c * SLOTS, SLOTS), where] = got[:SLOTS]
                outbox[pl.ds(c * SLOTS, SLOTS), where] = got[PAD : PAD + SLOTS]
                return 0

            lax.fori_loop(0, tiles, body, 0)

    def expert(c):
        block = pl.ds(2 * c * SLOTS, 2 * SLOTS)

        def half(g, _):
            where = pl.ds(pl.multiple_of(g * group, group), group)
            pre = nn(rows[block, pl.ds(0, width)], upw[g])
            s = jax.nn.sigmoid(pre)
            hidden[block, where] = (pre * s).astype(BF16)
            grad_hidden = nt(rows[block, pl.ds(width, width)], dnw[g])
            grad_pre[:, where] = (grad_hidden * s * (1.0 + pre * (1.0 - s))).astype(BF16)
            return 0

        lax.fori_loop(0, 2, half, 0)

        def body(j, _):
            where = columns(j)
            total = nt(grad_pre[:, pl.ds(0, group)], upw[0, where, :]) + nt(
                grad_pre[:, pl.ds(group, group)], upw[1, where, :]
            )
            pieces[block, where] = total.astype(BF16)
            return 0

        lax.fori_loop(0, tiles, body, 0)

    def scatter(c, half, extras, store):
        tokens = pl.ds(half * TOK, TOK)

        def body(j, _):
            where = columns(j)
            total = nn(picks[c, tokens, pl.ds(0, SLOTS)], pieces[pl.ds(2 * c * SLOTS, SLOTS), where])
            total += nn(picks[c, tokens, pl.ds(PAD, SLOTS)], back[pl.ds(c * SLOTS, SLOTS), where])
            for extra in extras:
                total += retin[extra, :, where].astype(F32)
            ret[store, :, where] = total.astype(BF16)
            return 0

        lax.fori_loop(0, tiles, body, 0)

    start(KEPT_UP)
    start(KEPT_DN)
    start(SWAP)
    own = pltpu.make_async_copy(kept, tok.at[0, first], local_sem.at[0])
    own.start()

    @pl.when(stay)
    def _():
        one = pltpu.make_async_copy(up, upw.at[0], local_sem.at[1])
        two = pltpu.make_async_copy(down, dnw.at[0], local_sem.at[2])
        one.start()
        two.start()
        one.wait()
        two.wait()
        copies[UP_B].start()
        copies[DOWN_B].start()

    arrived(SWAP)
    start(SWAPPED_UP)
    start(SWAPPED_DN)

    @pl.when(leave)
    def _():
        copies[UP_A].start()
        copies[DOWN_A].start()

    own.wait()
    pack(0)
    start(PACKED)
    arrived(KEPT_UP)
    start(FAR_KEPT)
    arrived(KEPT_DN)
    pack(1)
    start(PACKED + 1)
    arrived(SWAPPED_DN)
    start(FAR_SWAPPED)
    arrived(SWAPPED_UP)
    pack(2)
    start(PACKED + 2)

    @pl.when(leave)
    def _():
        copies[UP_A].wait()
        copies[DOWN_A].wait()
        copies[UP_B].start()
        copies[DOWN_B].start()

    sent_copies.extend([UP_B, DOWN_B])
    arrived(UP_B)
    arrived(DOWN_B)
    arrived(PACKED)
    expert(0)
    start(BACK)
    arrived(FAR_KEPT)
    arrived(FAR_SWAPPED)
    pack(3)
    start(PACKED + 3)
    arrived(PACKED + 1)
    expert(1)
    start(BACK + 1)
    arrived(PACKED + 2)
    expert(2)
    start(BACK + 2)
    arrived(BACK + 1)
    scatter(1, 1, (), 2)
    start(SUM_ABOVE_KEPT)
    arrived(BACK + 2)
    scatter(2, 0, (), 3)
    start(SUM_BELOW_SWAPPED)
    arrived(PACKED + 3)
    expert(3)
    start(BACK + 3)

    def mirrored(j):
        return pltpu.make_async_remote_copy(
            src_ref=part.at[:, columns(j)], dst_ref=mirror.at[:, columns(j)],
            send_sem=send_sem.at[MIRROR + j], recv_sem=recv_sem.at[MIRROR + j],
            device_id=twin, device_id_type=MESH,
        )

    def home(j):
        return pltpu.make_async_remote_copy(
            src_ref=mirror.at[:, columns(j)], dst_ref=out_down.at[:, columns(j)],
            send_sem=send_sem.at[MIRROR + tiles + j], recv_sem=recv_sem.at[MIRROR + tiles + j],
            device_id=crossed, device_id_type=MESH,
        )

    def stays(j):
        return pltpu.make_async_copy(
            mirror.at[:, columns(j)], out_down.at[:, columns(j)], local_sem.at[3 + j]
        )

    def gradient(j, g):
        where = pl.ds(pl.multiple_of(width + j * tile, 128), tile)
        return tn(hidden[:, pl.ds(g * group, group)], rows[:, where])

    def theirs(j, _):
        part[:, columns(j)] = gradient(j, 1).astype(BF16)
        mirrored(j).start()
        return 0

    lax.fori_loop(0, tiles, theirs, 0)

    arrived(BACK + 3)
    scatter(3, 0, (), 0)
    start(SUM_FAR_KEPT)
    scatter(3, 1, (), 1)
    start(SUM_FAR_SWAPPED)

    def ours(j, _):
        value = gradient(j, 0).astype(BF16).astype(F32)
        mirrored(j).wait_recv()
        mirror[:, columns(j)] = (value + mirror[:, columns(j)].astype(F32)).astype(BF16)

        @pl.when(stay)
        def _():
            stays(j).start()

        @pl.when(leave)
        def _():
            home(j).start()

        return 0

    lax.fori_loop(0, tiles, ours, 0)

    arrived(SUM_FAR_KEPT)
    scatter(1, 0, (0,), 4)
    start(SUM_BELOW_KEPT)
    arrived(SUM_FAR_SWAPPED)
    scatter(2, 1, (1,), 5)
    start(SUM_ABOVE_SWAPPED)
    arrived(BACK)
    arrived(SUM_BELOW_SWAPPED)
    arrived(SUM_ABOVE_SWAPPED)
    scatter(0, 1, (3, 5), 6)
    start(RESULT)
    arrived(SUM_ABOVE_KEPT)
    arrived(SUM_BELOW_KEPT)
    scatter(0, 0, (2, 4), 7)
    result = pltpu.make_async_copy(ret.at[7], out_kept, local_sem.at[0])
    result.start()

    for index in sent_copies:
        copies[index].wait_send()

    def ended(j, _):
        mirrored(j).wait_send()

        @pl.when(stay)
        def _():
            stays(j).wait()

        @pl.when(leave)
        def _():
            home(j).wait()

        return 0

    lax.fori_loop(0, tiles, ended, 0)
    result.wait()
    arrived(RESULT)


def exchange(kept, sent, up, down):
    width, group = up.shape
    tile = 512 if width % 512 == 0 else 128
    tiles = width // tile
    copies = MIRROR + 2 * tiles
    return pl.pallas_call(
        functools.partial(kernel, width, group, tile),
        out_shape=[
            jax.ShapeDtypeStruct((TOK, width), BF16),
            jax.ShapeDtypeStruct((TOK, width), BF16),
            jax.ShapeDtypeStruct((group, width), BF16),
        ],
        in_specs=[pl.BlockSpec(memory_space=pl.ANY)] * 4,
        out_specs=[pl.BlockSpec(memory_space=pl.ANY)] * 3,
        scratch_shapes=[
            pltpu.VMEM((4, PAIR, 2 * width + PAD), BF16),
            pltpu.VMEM((4 * SLOTS, 2 * width), BF16),
            pltpu.VMEM((8 * SLOTS, 2 * width), BF16),
            pltpu.VMEM((8 * SLOTS, 2 * group), BF16),
            pltpu.VMEM((2 * SLOTS, 2 * group), BF16),
            pltpu.VMEM((4, PAIR, 2 * PAD), BF16),
            pltpu.VMEM((8 * SLOTS, width), BF16),
            pltpu.VMEM((4 * SLOTS, width), BF16),
            pltpu.VMEM((8, TOK, width), BF16),
            pltpu.VMEM((6, TOK, width), BF16),
            pltpu.VMEM((2, width, group), BF16),
            pltpu.VMEM((2, group, width), BF16),
            pltpu.VMEM((group, width), BF16),
            pltpu.VMEM((group, width), BF16),
            pltpu.SemaphoreType.DMA((copies,)),
            pltpu.SemaphoreType.DMA((copies,)),
            pltpu.SemaphoreType.DMA((3 + tiles,)),
        ],
        compiler_params=pltpu.CompilerParams(
            collective_id=0, has_side_effects=True, vmem_limit_bytes=62 * 1024 * 1024
        ),
    )(kept, sent, up, down)


def on_device(fx, fg, froutes, flogits, rx, rg, rroutes, rlogits, up_weight, down_weight):
    core = lax.axis_index("pipe") % 2
    y = lax.axis_index("expert") % NY
    front_stays = core == (y + 1) // 2 % 2
    both = []
    for x, g, routes, logits in ((fx, fg, froutes, flogits), (rx, rg, rroutes, rlogits)):
        rows_float, inv_rms, normed = normalize(x[0])
        gates = gate_table(routes[0], logits[0])
        chosen = (gates != 0).astype(jnp.int32)
        rank = (jnp.cumsum(chosen, axis=0) - chosen).astype(BF16)
        table = jnp.pad(jnp.concatenate([gates, rank], axis=1), ((0, 0), (0, PAD - 2 * EXPERTS)))
        both.append((rows_float, inv_rms, g[0], jnp.concatenate([normed, g[0], table], axis=1)))
    kept = jnp.where(front_stays, both[0][3], both[1][3])
    sent = jnp.where(front_stays, both[1][3], both[0][3])
    from_kept, from_sent, down_grad = exchange(kept, sent, up_weight[0], down_weight[0])
    results = []
    for stays, (rows_float, inv_rms, g, _) in zip((front_stays, ~front_stays), both):
        results.append(finish(rows_float, inv_rms, g, jnp.where(stays, from_kept, from_sent)))
    return (results[0][None], results[1][None], down_grad[None])


def solution(mesh):
    rows = P("pipe", "expert", None)
    return jax.shard_map(
        on_device,
        mesh=mesh,
        in_specs=(rows,) * 8 + (P("pipe", None, "expert"), rows),
        out_specs=(rows, rows, rows),
        check_vma=False,
    )
```

```python
import functools

import jax
import jax.numpy as jnp
from jax import lax
from jax.experimental import pallas as pl
from jax.experimental.pallas import tpu as pltpu
from jax.sharding import PartitionSpec as P

EXPERTS = 8
CAP = 36
NY = 4
NZ = 4
TOK = 64
PAIR = 2 * TOK
SLOTS = 80
PAD = 128

epsilon = 1e-06
MESH = pl.DeviceIdType.MESH
F32, BF16 = jnp.float32, jnp.bfloat16

(
    KEPT_UP, KEPT_DN, SWAPPED_UP, SWAPPED_DN, FAR_UP, FAR_DN, SWAP, PACKED, _PACKED_1, _PACKED_2, _PACKED_3, PARTS,
) = range(12)
UP_A, DOWN_A, UP_B, DOWN_B = range(2 * PARTS, 2 * PARTS + 4)
TILED = 2 * PARTS + 4
SUM_FAR_KEPT, SUM_FAR_SWAPPED, SUM_ABOVE_KEPT, SUM_BELOW_SWAPPED, SUM_BELOW_KEPT, SUM_ABOVE_SWAPPED = range(6)
RESULT = 6
BACK = 7
MIRROR = 11
HOME = 12
TILED_KINDS = 13


def gate_table(routes, logits):
    weights = jax.nn.sigmoid(logits.astype(F32))
    weights = (weights / jnp.sum(weights, axis=-1, keepdims=True)).astype(BF16)
    onehot = routes[..., None] == jnp.arange(EXPERTS, dtype=jnp.int32)
    picked = jnp.where(onehot, weights[..., None].astype(F32), F32(0.0))
    return jnp.sum(picked, axis=-2).astype(BF16)


def normalize(row_block):
    rows_float = row_block.astype(F32)
    inv_rms = lax.rsqrt(jnp.mean(rows_float * rows_float, axis=-1, keepdims=True) + epsilon)
    return (rows_float, inv_rms, (rows_float * inv_rms).astype(BF16))


def finish(rows_float, inv_rms, incoming, grad_normed):
    grad_normed = grad_normed.astype(F32)
    inner = jnp.sum(grad_normed * rows_float, axis=-1, keepdims=True) / rows_float.shape[-1]
    grad_rows = inv_rms * grad_normed - inv_rms * inv_rms * inv_rms * rows_float * inner
    return (incoming.astype(F32) + grad_rows).astype(BF16)


def tn(a, b):
    return lax.dot_general(a, b, (((0,), (0,)), ((), ())), preferred_element_type=F32)


def nt(a, b):
    return lax.dot_general(a, b, (((1,), (1,)), ((), ())), preferred_element_type=F32)


def nn(a, b):
    return lax.dot_general(a, b, (((1,), (0,)), ((), ())), preferred_element_type=F32)


def kernel(
    width, group, tile,
    kept, sent, up, down,
    out_kept, out_sent, out_down,
    tok, outbox, rows, hidden, grad_pre, picks, weighted, pieces, back, ret, retin, upw, dnw, part, mirror,
    send_sem, recv_sem, local_sem,
):
    tiles = width // tile
    pipe, place = lax.axis_index("pipe"), lax.axis_index("expert")
    core, y, z = pipe % 2, place % NY, place // NY
    served = ((y + 1) // 2) % 2
    stay = core == served
    leave = core != served
    mine, other = 2 * z + y // 2, 2 * z + 1 - y // 2
    twin = (pipe + 1 - 2 * core, place)
    beside = (pipe, z * NY + y + 1 - 2 * (y % 2))
    opposite = (pipe, z * NY + 3 - y)
    above = (pipe, ((z + 1) % NZ) * NY + y)
    below = (pipe, ((z + NZ - 1) % NZ) * NY + y)
    crossed = (twin[0], beside[1])

    barrier = pltpu.get_barrier_semaphore()
    for device in (twin, beside, opposite, above, below):
        pl.semaphore_signal(barrier, inc=1, device_id=device, device_id_type=MESH)

    @pl.when(leave)
    def _():
        pl.semaphore_signal(barrier, inc=1, device_id=crossed, device_id_type=MESH)
        pl.semaphore_wait(barrier, 6)

    @pl.when(stay)
    def _():
        pl.semaphore_wait(barrier, 5)

    def remote(index, src, dst, device):
        return pltpu.make_async_remote_copy(
            src_ref=src, dst_ref=dst, send_sem=send_sem.at[index], recv_sem=recv_sem.at[index],
            device_id=device, device_id_type=MESH,
        )

    def mine_of(c):
        return pl.ds(2 * c * SLOTS, SLOTS)

    def other_of(c):
        return pl.ds((2 * c + 1) * SLOTS, SLOTS)

    first, second = pl.ds(0, TOK), pl.ds(TOK, TOK)
    copies = {
        UP_A: remote(UP_A, up, upw.at[0], crossed),
        DOWN_A: remote(DOWN_A, down, dnw.at[0], crossed),
        UP_B: remote(UP_B, upw.at[0], upw.at[1], twin),
        DOWN_B: remote(DOWN_B, dnw.at[0], dnw.at[1], twin),
    }
    NORMED, GRADS = 0, PARTS
    for part_of, of, packed_of in (
        (NORMED, pl.ds(0, PAD + width), pl.ds(0, width)),
        (GRADS, pl.ds(PAD + width, width), pl.ds(width, width)),
    ):
        for name, src, dst, device in (
            (KEPT_UP, kept.at[:, of], tok.at[1, first, of], above),
            (KEPT_DN, kept.at[:, of], tok.at[1, second, of], below),
            (SWAP, sent.at[:, of], tok.at[0, second, of], beside),
            (SWAPPED_UP, tok.at[0, second, of], tok.at[2, first, of], above),
            (SWAPPED_DN, tok.at[0, second, of], tok.at[2, second, of], below),
            (FAR_UP, tok.at[1, first, of], tok.at[3, first, of], above),
            (FAR_DN, tok.at[2, second, of], tok.at[3, second, of], below),
        ):
            copies[part_of + name] = remote(part_of + name, src, dst, device)
        for c in range(4):
            copies[part_of + PACKED + c] = remote(
                part_of + PACKED + c,
                outbox.at[pl.ds(c * SLOTS, SLOTS), packed_of], rows.at[other_of(c), packed_of], opposite,
            )
    whole_copies = []

    def start(*names):
        for name in names:
            copies[name].start()
            whole_copies.append(name)

    def arrived(*names):
        for name in names:
            copies[name].wait_recv()

    def columns(j, offset=0):
        return pl.ds(pl.multiple_of(offset + j * tile, 128), tile)

    def tiled(kind, j):
        where = columns(j)
        if kind >= BACK and kind < BACK + 4:
            c = kind - BACK
            src, dst, device = pieces.at[other_of(c), where], back.at[pl.ds(c * SLOTS, SLOTS), where], opposite
        elif kind == MIRROR:
            src, dst, device = part.at[:, where], mirror.at[:, where], twin
        elif kind == HOME:
            src, dst, device = mirror.at[:, where], out_down.at[:, where], crossed
        elif kind == RESULT:
            src, dst, device = ret.at[RESULT, :, where], out_sent.at[:, where], beside
        else:
            src, dst = ret.at[kind, :, where], retin.at[kind, :, where]
            device = above if kind in (SUM_FAR_SWAPPED, SUM_ABOVE_KEPT, SUM_ABOVE_SWAPPED) else below
        return remote(TILED + kind * tiles + j, src, dst, device)

    def loop(step):
        def body(j, carry):
            step(j)
            return carry

        lax.fori_loop(0, tiles, body, 0)

    def matrices(c):
        table = tok[c, :, pl.ds(0, PAD)].astype(F32)
        lane = lax.broadcasted_iota(jnp.int32, (PAIR, PAD), 1)
        later = jnp.where(lax.broadcasted_iota(jnp.int32, (PAIR, 1), 0) >= TOK, F32(CAP), F32(0.0))
        plain, gates = [], []
        for expert in (mine, other):
            gate = jnp.sum(jnp.where(lane == expert, table, 0.0), axis=1, keepdims=True)
            rank = jnp.sum(jnp.where(lane == expert + EXPERTS, table, 0.0), axis=1, keepdims=True) + later
            hit = (gate != 0.0) & (rank == lane.astype(F32))
            plain.append(jnp.where(hit, 1.0, 0.0).astype(BF16))
            gates.append(jnp.where(hit, gate, 0.0).astype(BF16))
        return jnp.concatenate(plain, axis=1), jnp.concatenate(gates, axis=1)

    def pack_part(c, matrix, offset):
        def step(j):
            where = columns(j, offset)
            got = tn(matrix, tok[c, :, columns(j, PAD + offset)]).astype(BF16)
            rows[mine_of(c), where] = got[:SLOTS]
            outbox[pl.ds(c * SLOTS, SLOTS), where] = got[PAD : PAD + SLOTS]

        loop(step)

    def pack_normed(c):
        plain, gates = matrices(c)
        picks[c] = plain
        weighted[c] = gates
        pack_part(c, plain, 0)
        start(NORMED + PACKED + c)

    def pack_grads(c):
        pack_part(c, weighted[c], width)
        start(GRADS + PACKED + c)

    def activate(c):
        block = pl.ds(2 * c * SLOTS, 2 * SLOTS)

        def half(g, carry):
            where = pl.ds(pl.multiple_of(g * group, group), group)
            pre = nn(rows[block, pl.ds(0, width)], upw[g])
            s = jax.nn.sigmoid(pre)
            hidden[block, where] = (pre * s).astype(BF16)
            grad_hidden = nt(rows[block, pl.ds(width, width)], dnw[g])
            grad_pre[block, where] = (grad_hidden * s * (1.0 + pre * (1.0 - s))).astype(BF16)
            return carry

        lax.fori_loop(0, 2, half, 0)

    def piece(c):
        block = pl.ds(2 * c * SLOTS, 2 * SLOTS)

        def step(j):
            where = columns(j)
            total = nt(grad_pre[block, pl.ds(0, group)], upw[0, where, :]) + nt(
                grad_pre[block, pl.ds(group, group)], upw[1, where, :]
            )
            total = total.astype(BF16)
            pieces[other_of(c), where] = total[SLOTS:]
            tiled(BACK + c, j).start()
            pieces[mine_of(c), where] = total[:SLOTS]

        loop(step)

    def scatter(c, half, extras, store, awaited):
        tokens = pl.ds(half * TOK, TOK)

        def step(j):
            where = columns(j)
            for kind in awaited + extras:
                tiled(kind, j).wait_recv()
            total = nn(picks[c, tokens, pl.ds(0, SLOTS)], pieces[mine_of(c), where])
            total += nn(picks[c, tokens, pl.ds(PAD, SLOTS)], back[pl.ds(c * SLOTS, SLOTS), where])
            for extra in extras:
                total += retin[extra, :, where].astype(F32)
            ret[store, :, where] = total.astype(BF16)
            if store <= RESULT:
                tiled(store, j).start()

        loop(step)

    start(NORMED + KEPT_UP, NORMED + KEPT_DN, NORMED + SWAP)
    own = pltpu.make_async_copy(kept, tok.at[0, first], local_sem.at[0])
    own.start()

    @pl.when(stay)
    def _():
        one = pltpu.make_async_copy(up, upw.at[0], local_sem.at[1])
        two = pltpu.make_async_copy(down, dnw.at[0], local_sem.at[2])
        one.start()
        two.start()
        one.wait()
        two.wait()
        copies[UP_B].start()
        copies[DOWN_B].start()

    arrived(NORMED + SWAP)
    start(NORMED + SWAPPED_UP, NORMED + SWAPPED_DN, GRADS + SWAP)
    own.wait()
    pack_normed(0)
    arrived(NORMED + KEPT_UP)
    start(NORMED + FAR_UP)
    arrived(NORMED + KEPT_DN)
    pack_normed(1)
    arrived(GRADS + SWAP)

    @pl.when(leave)
    def _():
        copies[UP_A].start()

    pack_grads(0)
    arrived(NORMED + SWAPPED_DN)
    start(NORMED + FAR_DN, GRADS + KEPT_DN)
    arrived(NORMED + SWAPPED_UP)
    start(GRADS + KEPT_UP)

    @pl.when(leave)
    def _():
        copies[DOWN_A].start()

    pack_normed(2)
    arrived(NORMED + FAR_UP)
    start(GRADS + SWAPPED_UP)
    arrived(NORMED + FAR_DN)
    start(GRADS + SWAPPED_DN)
    pack_normed(3)
    arrived(GRADS + KEPT_UP)
    start(GRADS + FAR_UP)
    arrived(GRADS + KEPT_DN)
    pack_grads(1)

    @pl.when(leave)
    def _():
        copies[UP_A].wait()
        copies[UP_B].start()

    arrived(GRADS + SWAPPED_DN)
    start(GRADS + FAR_DN)
    arrived(GRADS + SWAPPED_UP)
    pack_grads(2)

    @pl.when(leave)
    def _():
        copies[DOWN_A].wait()
        copies[DOWN_B].start()

    arrived(UP_B, DOWN_B)
    arrived(NORMED + PACKED + 1, GRADS + PACKED + 1)
    activate(1)
    piece(1)
    arrived(GRADS + FAR_UP, GRADS + FAR_DN)
    pack_grads(3)
    arrived(NORMED + PACKED, GRADS + PACKED)
    activate(0)
    arrived(NORMED + PACKED + 2, GRADS + PACKED + 2)
    activate(2)
    scatter(1, 1, (), SUM_ABOVE_KEPT, (BACK + 1,))
    arrived(NORMED + PACKED + 3, GRADS + PACKED + 3)
    piece(2)

    def gradient(j, g):
        return tn(hidden[:, pl.ds(g * group, group)], rows[:, columns(j, width)])

    def theirs(j):
        part[:, columns(j)] = gradient(j, 1).astype(BF16)
        tiled(MIRROR, j).start()

    def stays(j):
        return pltpu.make_async_copy(mirror.at[:, columns(j)], out_down.at[:, columns(j)], local_sem.at[3 + j])

    def ours(j):
        value = gradient(j, 0).astype(BF16).astype(F32)
        tiled(MIRROR, j).wait_recv()
        mirror[:, columns(j)] = (value + mirror[:, columns(j)].astype(F32)).astype(BF16)

        @pl.when(stay)
        def _():
            stays(j).start()

        @pl.when(leave)
        def _():
            tiled(HOME, j).start()

    activate(3)
    loop(theirs)
    piece(3)
    loop(ours)
    scatter(3, 0, (), SUM_FAR_KEPT, (BACK + 3,))
    scatter(3, 1, (), SUM_FAR_SWAPPED, ())
    piece(0)
    scatter(2, 0, (), SUM_BELOW_SWAPPED, (BACK + 2,))
    scatter(1, 0, (SUM_FAR_KEPT,), SUM_BELOW_KEPT, ())
    scatter(2, 1, (SUM_FAR_SWAPPED,), SUM_ABOVE_SWAPPED, ())
    scatter(0, 1, (SUM_BELOW_SWAPPED, SUM_ABOVE_SWAPPED), RESULT, (BACK,))
    scatter(0, 0, (SUM_ABOVE_KEPT, SUM_BELOW_KEPT), RESULT + 1, ())
    result = pltpu.make_async_copy(ret.at[RESULT + 1], out_kept, local_sem.at[0])
    result.start()

    for name in whole_copies + [UP_B, DOWN_B]:
        copies[name].wait_send()

    def ended(j):
        for kind in range(HOME):
            tiled(kind, j).wait_send()
        tiled(RESULT, j).wait_recv()

        @pl.when(stay)
        def _():
            stays(j).wait()

        @pl.when(leave)
        def _():
            tiled(HOME, j).wait()

    loop(ended)
    result.wait()


def exchange(kept, sent, up, down):
    width, group = up.shape
    tile = 512 if width % 512 == 0 else 128
    tiles = width // tile
    copies = TILED + TILED_KINDS * tiles
    return pl.pallas_call(
        functools.partial(kernel, width, group, tile),
        out_shape=[
            jax.ShapeDtypeStruct((TOK, width), BF16),
            jax.ShapeDtypeStruct((TOK, width), BF16),
            jax.ShapeDtypeStruct((group, width), BF16),
        ],
        in_specs=[pl.BlockSpec(memory_space=pl.ANY)] * 4,
        out_specs=[pl.BlockSpec(memory_space=pl.ANY)] * 3,
        scratch_shapes=[
            pltpu.VMEM((4, PAIR, 2 * width + PAD), BF16),
            pltpu.VMEM((4 * SLOTS, 2 * width), BF16),
            pltpu.VMEM((8 * SLOTS, 2 * width), BF16),
            pltpu.VMEM((8 * SLOTS, 2 * group), BF16),
            pltpu.VMEM((8 * SLOTS, 2 * group), BF16),
            pltpu.VMEM((4, PAIR, 2 * PAD), BF16),
            pltpu.VMEM((4, PAIR, 2 * PAD), BF16),
            pltpu.VMEM((8 * SLOTS, width), BF16),
            pltpu.VMEM((4 * SLOTS, width), BF16),
            pltpu.VMEM((8, TOK, width), BF16),
            pltpu.VMEM((6, TOK, width), BF16),
            pltpu.VMEM((2, width, group), BF16),
            pltpu.VMEM((2, group, width), BF16),
            pltpu.VMEM((group, width), BF16),
            pltpu.VMEM((group, width), BF16),
            pltpu.SemaphoreType.DMA((copies,)),
            pltpu.SemaphoreType.DMA((copies,)),
            pltpu.SemaphoreType.DMA((3 + tiles,)),
        ],
        compiler_params=pltpu.CompilerParams(
            collective_id=0, has_side_effects=True, vmem_limit_bytes=62 * 1024 * 1024
        ),
    )(kept, sent, up, down)


def on_device(fx, fg, froutes, flogits, rx, rg, rroutes, rlogits, up_weight, down_weight):
    core = lax.axis_index("pipe") % 2
    y = lax.axis_index("expert") % NY
    front_stays = core == (y + 1) // 2 % 2
    both = []
    for x, g, routes, logits in ((fx, fg, froutes, flogits), (rx, rg, rroutes, rlogits)):
        rows_float, inv_rms, normed = normalize(x[0])
        gates = gate_table(routes[0], logits[0])
        chosen = (gates != 0).astype(jnp.int32)
        rank = (jnp.cumsum(chosen, axis=0) - chosen).astype(BF16)
        table = jnp.pad(jnp.concatenate([gates, rank], axis=1), ((0, 0), (0, PAD - 2 * EXPERTS)))
        both.append((rows_float, inv_rms, g[0], jnp.concatenate([table, normed, g[0]], axis=1)))
    kept = jnp.where(front_stays, both[0][3], both[1][3])
    sent = jnp.where(front_stays, both[1][3], both[0][3])
    from_kept, from_sent, down_grad = exchange(kept, sent, up_weight[0], down_weight[0])
    results = []
    for stays, (rows_float, inv_rms, g, _) in zip((front_stays, ~front_stays), both):
        results.append(finish(rows_float, inv_rms, g, jnp.where(stays, from_kept, from_sent)))
    return (results[0][None], results[1][None], down_grad[None])


def solution(mesh):
    rows = P("pipe", "expert", None)
    return jax.shard_map(
        on_device,
        mesh=mesh,
        in_specs=(rows,) * 8 + (P("pipe", None, "expert"), rows),
        out_specs=(rows, rows, rows),
        check_vma=False,
    )
```

```python
import functools

import jax
import jax.numpy as jnp
from jax import lax
from jax.experimental import pallas as pl
from jax.experimental.pallas import tpu as pltpu
from jax.sharding import PartitionSpec as P

EXPERTS = 8
CAP = 36
NY = 4
NZ = 4
TOK = 64
PAIR = 2 * TOK
SLOTS = 80
PAD = 128

epsilon = 1e-06
MESH = pl.DeviceIdType.MESH
F32, BF16 = jnp.float32, jnp.bfloat16

(
    KEPT_UP, KEPT_DN, SWAPPED_UP, SWAPPED_DN, FAR_UP, FAR_DN, SWAP, PACKED, _PACKED_1, _PACKED_2, _PACKED_3, PARTS,
) = range(12)
UP_A, DOWN_A, UP_B, DOWN_B = range(2 * PARTS, 2 * PARTS + 4)
TILED = 2 * PARTS + 4
SUM_FAR_KEPT, SUM_FAR_SWAPPED, SUM_ABOVE_KEPT, SUM_BELOW_SWAPPED, SUM_BELOW_KEPT, SUM_ABOVE_SWAPPED = range(6)
RESULT = 6
BACK = 7
MIRROR = 11
HOME = 12
TILED_KINDS = 13


def gate_table(routes, logits):
    weights = jax.nn.sigmoid(logits.astype(F32))
    weights = (weights / jnp.sum(weights, axis=-1, keepdims=True)).astype(BF16)
    onehot = routes[..., None] == jnp.arange(EXPERTS, dtype=jnp.int32)
    picked = jnp.where(onehot, weights[..., None].astype(F32), F32(0.0))
    return jnp.sum(picked, axis=-2).astype(BF16)


def normalize(row_block):
    rows_float = row_block.astype(F32)
    inv_rms = lax.rsqrt(jnp.mean(rows_float * rows_float, axis=-1, keepdims=True) + epsilon)
    return (rows_float, inv_rms, (rows_float * inv_rms).astype(BF16))


def finish(rows_float, inv_rms, incoming, grad_normed):
    grad_normed = grad_normed.astype(F32)
    inner = jnp.sum(grad_normed * rows_float, axis=-1, keepdims=True) / rows_float.shape[-1]
    grad_rows = inv_rms * grad_normed - inv_rms * inv_rms * inv_rms * rows_float * inner
    return (incoming.astype(F32) + grad_rows).astype(BF16)


def tn(a, b):
    return lax.dot_general(a, b, (((0,), (0,)), ((), ())), preferred_element_type=F32)


def nt(a, b):
    return lax.dot_general(a, b, (((1,), (1,)), ((), ())), preferred_element_type=F32)


def nn(a, b):
    return lax.dot_general(a, b, (((1,), (0,)), ((), ())), preferred_element_type=F32)


def kernel(
    width, group, tile,
    kept, sent, up, down,
    out_kept, out_sent, out_down,
    tok, outbox, rows, hidden, grad_pre, picks, weighted, pieces, back, ret, retin, upw, dnw, part, mirror,
    send_sem, recv_sem, local_sem,
):
    tiles = width // tile
    pipe, place = lax.axis_index("pipe"), lax.axis_index("expert")
    core, y, z = pipe % 2, place % NY, place // NY
    served = ((y + 1) // 2) % 2
    stay = core == served
    leave = core != served
    mine, other = 2 * z + y // 2, 2 * z + 1 - y // 2
    twin = (pipe + 1 - 2 * core, place)
    beside = (pipe, z * NY + y + 1 - 2 * (y % 2))
    opposite = (pipe, z * NY + 3 - y)
    above = (pipe, ((z + 1) % NZ) * NY + y)
    below = (pipe, ((z + NZ - 1) % NZ) * NY + y)
    crossed = (twin[0], beside[1])

    barrier = pltpu.get_barrier_semaphore()
    for device in (twin, beside, opposite, above, below):
        pl.semaphore_signal(barrier, inc=1, device_id=device, device_id_type=MESH)

    @pl.when(leave)
    def _():
        pl.semaphore_signal(barrier, inc=1, device_id=crossed, device_id_type=MESH)
        pl.semaphore_wait(barrier, 6)

    @pl.when(stay)
    def _():
        pl.semaphore_wait(barrier, 5)

    def remote(index, src, dst, device):
        return pltpu.make_async_remote_copy(
            src_ref=src, dst_ref=dst, send_sem=send_sem.at[index], recv_sem=recv_sem.at[index],
            device_id=device, device_id_type=MESH,
        )

    def mine_of(c):
        return pl.ds(2 * c * SLOTS, SLOTS)

    def other_of(c):
        return pl.ds((2 * c + 1) * SLOTS, SLOTS)

    first, second = pl.ds(0, TOK), pl.ds(TOK, TOK)
    copies = {
        UP_A: remote(UP_A, up, upw.at[0], crossed),
        DOWN_A: remote(DOWN_A, down, dnw.at[0], crossed),
        UP_B: remote(UP_B, upw.at[0], upw.at[1], twin),
        DOWN_B: remote(DOWN_B, dnw.at[0], dnw.at[1], twin),
    }
    NORMED, GRADS = 0, PARTS
    for part_of, of, packed_of in (
        (NORMED, pl.ds(0, PAD + width), pl.ds(0, width)),
        (GRADS, pl.ds(PAD + width, width), pl.ds(width, width)),
    ):
        for name, src, dst, device in (
            (KEPT_UP, kept.at[:, of], tok.at[1, first, of], above),
            (KEPT_DN, kept.at[:, of], tok.at[1, second, of], below),
            (SWAP, sent.at[:, of], tok.at[0, second, of], beside),
            (SWAPPED_UP, tok.at[0, second, of], tok.at[2, first, of], above),
            (SWAPPED_DN, tok.at[0, second, of], tok.at[2, second, of], below),
            (FAR_UP, tok.at[1, first, of], tok.at[3, first, of], above),
            (FAR_DN, tok.at[2, second, of], tok.at[3, second, of], below),
        ):
            copies[part_of + name] = remote(part_of + name, src, dst, device)
        for c in range(4):
            copies[part_of + PACKED + c] = remote(
                part_of + PACKED + c,
                outbox.at[pl.ds(c * SLOTS, SLOTS), packed_of], rows.at[other_of(c), packed_of], opposite,
            )
    whole_copies = []

    def start(*names):
        for name in names:
            copies[name].start()
            whole_copies.append(name)

    def arrived(*names):
        for name in names:
            copies[name].wait_recv()

    def columns(j, offset=0):
        return pl.ds(pl.multiple_of(offset + j * tile, 128), tile)

    def tiled(kind, j):
        where = columns(j)
        if kind >= BACK and kind < BACK + 4:
            c = kind - BACK
            src, dst, device = pieces.at[other_of(c), where], back.at[pl.ds(c * SLOTS, SLOTS), where], opposite
        elif kind == MIRROR:
            src, dst, device = part.at[:, where], mirror.at[:, where], twin
        elif kind == HOME:
            src, dst, device = mirror.at[:, where], out_down.at[:, where], crossed
        elif kind == RESULT:
            src, dst, device = ret.at[RESULT, :, where], out_sent.at[:, where], beside
        else:
            src, dst = ret.at[kind, :, where], retin.at[kind, :, where]
            device = above if kind in (SUM_FAR_SWAPPED, SUM_ABOVE_KEPT, SUM_ABOVE_SWAPPED) else below
        return remote(TILED + kind * tiles + j, src, dst, device)

    def loop(step):
        def body(j, carry):
            step(j)
            return carry

        lax.fori_loop(0, tiles, body, 0)

    def matrices(c):
        table = tok[c, :, pl.ds(0, PAD)].astype(F32)
        lane = lax.broadcasted_iota(jnp.int32, (PAIR, PAD), 1)
        later = jnp.where(lax.broadcasted_iota(jnp.int32, (PAIR, 1), 0) >= TOK, F32(CAP), F32(0.0))
        plain, gates = [], []
        for expert in (mine, other):
            gate = jnp.sum(jnp.where(lane == expert, table, 0.0), axis=1, keepdims=True)
            rank = jnp.sum(jnp.where(lane == expert + EXPERTS, table, 0.0), axis=1, keepdims=True) + later
            hit = (gate != 0.0) & (rank == lane.astype(F32))
            plain.append(jnp.where(hit, 1.0, 0.0).astype(BF16))
            gates.append(jnp.where(hit, gate, 0.0).astype(BF16))
        return jnp.concatenate(plain, axis=1), jnp.concatenate(gates, axis=1)

    def pack_part(c, matrix, offset):
        def step(j):
            where = columns(j, offset)
            got = tn(matrix, tok[c, :, columns(j, PAD + offset)]).astype(BF16)
            rows[mine_of(c), where] = got[:SLOTS]
            outbox[pl.ds(c * SLOTS, SLOTS), where] = got[PAD : PAD + SLOTS]

        loop(step)

    def pack_normed(c):
        plain, gates = matrices(c)
        picks[c] = plain
        weighted[c] = gates
        pack_part(c, plain, 0)
        start(NORMED + PACKED + c)

    def pack_grads(c):
        pack_part(c, weighted[c], width)
        start(GRADS + PACKED + c)

    def activate(c):
        block = pl.ds(2 * c * SLOTS, 2 * SLOTS)

        def half(g, carry):
            where = pl.ds(pl.multiple_of(g * group, group), group)
            pre = nn(rows[block, pl.ds(0, width)], upw[g])
            s = jax.nn.sigmoid(pre)
            hidden[block, where] = (pre * s).astype(BF16)
            grad_hidden = nt(rows[block, pl.ds(width, width)], dnw[g])
            grad_pre[block, where] = (grad_hidden * s * (1.0 + pre * (1.0 - s))).astype(BF16)
            return carry

        lax.fori_loop(0, 2, half, 0)

    def piece(c):
        block = pl.ds(2 * c * SLOTS, 2 * SLOTS)

        def step(j):
            where = columns(j)
            total = nt(grad_pre[block, pl.ds(0, group)], upw[0, where, :]) + nt(
                grad_pre[block, pl.ds(group, group)], upw[1, where, :]
            )
            total = total.astype(BF16)
            pieces[other_of(c), where] = total[SLOTS:]
            tiled(BACK + c, j).start()
            pieces[mine_of(c), where] = total[:SLOTS]

        loop(step)

    def scatter(c, half, extras, store, awaited):
        tokens = pl.ds(half * TOK, TOK)

        def step(j):
            where = columns(j)
            for kind in awaited + extras:
                tiled(kind, j).wait_recv()
            total = nn(picks[c, tokens, pl.ds(0, SLOTS)], pieces[mine_of(c), where])
            total += nn(picks[c, tokens, pl.ds(PAD, SLOTS)], back[pl.ds(c * SLOTS, SLOTS), where])
            for extra in extras:
                total += retin[extra, :, where].astype(F32)
            ret[store, :, where] = total.astype(BF16)
            if store <= RESULT:
                tiled(store, j).start()

        loop(step)

    start(NORMED + KEPT_UP, NORMED + KEPT_DN, NORMED + SWAP)
    own = pltpu.make_async_copy(kept, tok.at[0, first], local_sem.at[0])
    own.start()

    @pl.when(stay)
    def _():
        one = pltpu.make_async_copy(up, upw.at[0], local_sem.at[1])
        two = pltpu.make_async_copy(down, dnw.at[0], local_sem.at[2])
        one.start()
        two.start()
        one.wait()
        two.wait()
        copies[UP_B].start()
        copies[DOWN_B].start()

    arrived(NORMED + SWAP)
    start(NORMED + SWAPPED_UP, NORMED + SWAPPED_DN, GRADS + SWAP)
    own.wait()
    pack_normed(0)
    arrived(NORMED + KEPT_UP)
    start(NORMED + FAR_UP)
    arrived(NORMED + KEPT_DN)
    pack_normed(1)
    arrived(GRADS + SWAP)

    @pl.when(leave)
    def _():
        copies[UP_A].start()

    pack_grads(0)
    arrived(NORMED + SWAPPED_DN)
    start(NORMED + FAR_DN, GRADS + KEPT_DN)
    arrived(NORMED + SWAPPED_UP)
    start(GRADS + KEPT_UP)

    @pl.when(leave)
    def _():
        copies[DOWN_A].start()

    pack_normed(2)
    arrived(NORMED + FAR_UP)
    start(GRADS + SWAPPED_UP)
    arrived(NORMED + FAR_DN)
    start(GRADS + SWAPPED_DN)
    pack_normed(3)
    arrived(GRADS + KEPT_UP)
    start(GRADS + FAR_UP)
    arrived(GRADS + KEPT_DN)
    pack_grads(1)

    @pl.when(leave)
    def _():
        copies[UP_A].wait()
        copies[UP_B].start()

    arrived(GRADS + SWAPPED_DN)
    start(GRADS + FAR_DN)
    arrived(GRADS + SWAPPED_UP)
    pack_grads(2)

    @pl.when(leave)
    def _():
        copies[DOWN_A].wait()
        copies[DOWN_B].start()

    arrived(UP_B, DOWN_B)
    arrived(NORMED + PACKED + 1, GRADS + PACKED + 1)
    activate(1)
    piece(1)
    arrived(GRADS + FAR_UP, GRADS + FAR_DN)
    pack_grads(3)
    arrived(NORMED + PACKED, GRADS + PACKED)
    activate(0)
    arrived(NORMED + PACKED + 2, GRADS + PACKED + 2)
    activate(2)
    scatter(1, 1, (), SUM_ABOVE_KEPT, (BACK + 1,))
    arrived(NORMED + PACKED + 3, GRADS + PACKED + 3)
    piece(2)

    def gradient(j, g):
        return tn(hidden[:, pl.ds(g * group, group)], rows[:, columns(j, width)])

    def theirs(j):
        part[:, columns(j)] = gradient(j, 1).astype(BF16)
        tiled(MIRROR, j).start()

    def stays(j):
        return pltpu.make_async_copy(mirror.at[:, columns(j)], out_down.at[:, columns(j)], local_sem.at[3 + j])

    def ours(j):
        value = gradient(j, 0).astype(BF16).astype(F32)
        tiled(MIRROR, j).wait_recv()
        mirror[:, columns(j)] = (value + mirror[:, columns(j)].astype(F32)).astype(BF16)

        @pl.when(stay)
        def _():
            stays(j).start()

        @pl.when(leave)
        def _():
            tiled(HOME, j).start()

    activate(3)
    loop(theirs)
    piece(3)
    loop(ours)
    scatter(3, 0, (), SUM_FAR_KEPT, (BACK + 3,))
    scatter(3, 1, (), SUM_FAR_SWAPPED, ())
    piece(0)
    scatter(2, 0, (), SUM_BELOW_SWAPPED, (BACK + 2,))
    scatter(1, 0, (SUM_FAR_KEPT,), SUM_BELOW_KEPT, ())
    scatter(2, 1, (SUM_FAR_SWAPPED,), SUM_ABOVE_SWAPPED, ())
    scatter(0, 1, (SUM_BELOW_SWAPPED, SUM_ABOVE_SWAPPED), RESULT, (BACK,))
    scatter(0, 0, (SUM_ABOVE_KEPT, SUM_BELOW_KEPT), RESULT + 1, ())
    result = pltpu.make_async_copy(ret.at[RESULT + 1], out_kept, local_sem.at[0])
    result.start()

    for name in whole_copies + [UP_B, DOWN_B]:
        copies[name].wait_send()

    def ended(j):
        for kind in range(HOME):
            tiled(kind, j).wait_send()
        tiled(RESULT, j).wait_recv()

        @pl.when(stay)
        def _():
            stays(j).wait()

        @pl.when(leave)
        def _():
            tiled(HOME, j).wait()

    loop(ended)
    result.wait()


def exchange(kept, sent, up, down):
    width, group = up.shape
    tile = 896 if width % 896 == 0 else 128
    tiles = width // tile
    copies = TILED + TILED_KINDS * tiles
    return pl.pallas_call(
        functools.partial(kernel, width, group, tile),
        out_shape=[
            jax.ShapeDtypeStruct((TOK, width), BF16),
            jax.ShapeDtypeStruct((TOK, width), BF16),
            jax.ShapeDtypeStruct((group, width), BF16),
        ],
        in_specs=[pl.BlockSpec(memory_space=pl.ANY)] * 4,
        out_specs=[pl.BlockSpec(memory_space=pl.ANY)] * 3,
        scratch_shapes=[
            pltpu.VMEM((4, PAIR, 2 * width + PAD), BF16),
            pltpu.VMEM((4 * SLOTS, 2 * width), BF16),
            pltpu.VMEM((8 * SLOTS, 2 * width), BF16),
            pltpu.VMEM((8 * SLOTS, 2 * group), BF16),
            pltpu.VMEM((8 * SLOTS, 2 * group), BF16),
            pltpu.VMEM((4, PAIR, 2 * PAD), BF16),
            pltpu.VMEM((4, PAIR, 2 * PAD), BF16),
            pltpu.VMEM((8 * SLOTS, width), BF16),
            pltpu.VMEM((4 * SLOTS, width), BF16),
            pltpu.VMEM((8, TOK, width), BF16),
            pltpu.VMEM((6, TOK, width), BF16),
            pltpu.VMEM((2, width, group), BF16),
            pltpu.VMEM((2, group, width), BF16),
            pltpu.VMEM((group, width), BF16),
            pltpu.VMEM((group, width), BF16),
            pltpu.SemaphoreType.DMA((copies,)),
            pltpu.SemaphoreType.DMA((copies,)),
            pltpu.SemaphoreType.DMA((3 + tiles,)),
        ],
        compiler_params=pltpu.CompilerParams(
            collective_id=0, has_side_effects=True, vmem_limit_bytes=62 * 1024 * 1024
        ),
    )(kept, sent, up, down)


def on_device(fx, fg, froutes, flogits, rx, rg, rroutes, rlogits, up_weight, down_weight):
    core = lax.axis_index("pipe") % 2
    y = lax.axis_index("expert") % NY
    front_stays = core == (y + 1) // 2 % 2
    both = []
    for x, g, routes, logits in ((fx, fg, froutes, flogits), (rx, rg, rroutes, rlogits)):
        rows_float, inv_rms, normed = normalize(x[0])
        gates = gate_table(routes[0], logits[0])
        chosen = (gates != 0).astype(jnp.int32)
        rank = (jnp.cumsum(chosen, axis=0) - chosen).astype(BF16)
        table = jnp.pad(jnp.concatenate([gates, rank], axis=1), ((0, 0), (0, PAD - 2 * EXPERTS)))
        both.append((rows_float, inv_rms, g[0], jnp.concatenate([table, normed, g[0]], axis=1)))
    kept = jnp.where(front_stays, both[0][3], both[1][3])
    sent = jnp.where(front_stays, both[1][3], both[0][3])
    from_kept, from_sent, down_grad = exchange(kept, sent, up_weight[0], down_weight[0])
    results = []
    for stays, (rows_float, inv_rms, g, _) in zip((front_stays, ~front_stays), both):
        results.append(finish(rows_float, inv_rms, g, jnp.where(stays, from_kept, from_sent)))
    return (results[0][None], results[1][None], down_grad[None])


def solution(mesh):
    rows = P("pipe", "expert", None)
    return jax.shard_map(
        on_device,
        mesh=mesh,
        in_specs=(rows,) * 8 + (P("pipe", None, "expert"), rows),
        out_specs=(rows, rows, rows),
        check_vma=False,
    )
```
